32 devices in a mesh: expert: 4 (over x, core), shard: 8 (over z, y).
Axes of the slice: x: 2, y: 2, z: 4, core: 2. Of those that a mesh axis runs over, the one named last changes fastest.
Arguments:
- tokens: bfloat16 [8, 1024, 768], P('shard', 'expert'), may hold values from -22 to 22
- w_query: bfloat16 [768, 768], P('shard'), may hold values from -0.21875 to 0.21875
- w_key: bfloat16 [768, 768], P('shard'), may hold values from -0.21875 to 0.21875
- w_value: bfloat16 [768, 768], P('shard'), may hold values from -0.21875 to 0.21875
- w_output: bfloat16 [768, 768], P('shard'), may hold values from -2.5 to 2.5
- w_router: bfloat16 [768, 4], P('shard'), may hold values from -0.15625 to 0.15625
- norm_one: bfloat16 [768], P('shard'), may hold values from 0.5 to 1.5
- norm_two: bfloat16 [768], P('shard'), may hold values from 0.5 to 1.5
- rel_bias: bfloat16 [32, 12], P('shard'), may hold values from -4 to 4
- w_in: bfloat16 [4, 768, 3072], P('expert'), may hold values from -0.21875 to 0.21875
- w_out: bfloat16 [4, 3072, 768], P('expert'), may hold values from -1.25 to 1.25
- routes: int32 [8, 1024, 1], P('shard', 'expert'), may hold values from 0 to 3; in each aligned block of 256 rows (0 to 255, 256 to 511, ..., all dimensions but the last counted through in order) at most 128 rows name the same one
- seq_ids: int32 [8, 1024], P('shard'), may hold values from 0 to 2, as said below
- buckets: int32 [2047], replicated, may hold values from 0 to 31
- d_out: bfloat16 [8, 1024, 768], P('shard', 'expert'), may hold values from -6 to 6
Outputs:
- layer_out: bfloat16 [8, 1024, 768], P('shard', 'expert')
- d_tokens: float32 [8, 1024, 768], P('shard', 'expert')
- d_w_query: float32 [768, 768], P('shard')
- d_w_key: float32 [768, 768], P('shard')
- d_w_value: float32 [768, 768], P('shard')
- d_w_output: float32 [768, 768], P('shard')
- d_w_router: float32 [768, 4], P('shard')
- d_norm_one: float32 [768], P('shard')
- d_norm_two: float32 [768], P('shard')
- d_rel_bias: float32 [32, 12], P('shard')
- d_w_in: float32 [4, 768, 3072], P('expert', 'shard')
- d_w_out: float32 [4, 3072, 768], P('expert', 'shard')
The draws below stay inside these ranges and needn't reach their ends.
Inputs may be any that keep to these rules, and one draw needn't show every extreme that they name: `routes`: among the rows of one device no expert is named more than 128 times, and in some device's rows one expert is named exactly 128 times. `seq_ids`: ids never fall along a sequence, and every sequence holds ids 0, 1 and 2.
All inputs are finite; a program needn't handle non-finite values.
Results may differ from the reference program's by a relative error of at most 0.04.
Values may be sent and summed in bfloat16 or wider, within the bound.
A program may use at most 192 MiB of HBM per device.

```python
import math
import jax
import jax.numpy as jnp
import numpy as np
from jax import lax

D = 768
H = 12
HD = 64
FF = 3072
NB = 32
LEN = 1024
EXPERTS = 4
SEQS = 8
TOK_DEV = 256
CAP = 128


def draw_tokens(key, part):
    key = jax.random.fold_in(key, 11)
    base_key, row_key, col_key = jax.random.split(key, 3)
    row_scale = jnp.exp(jax.random.uniform(row_key, (SEQS, LEN, 1), jnp.float32, math.log(0.3), math.log(3.0)))
    col_scale = jnp.exp(jax.random.uniform(col_key, (1, 1, D), jnp.float32, math.log(0.6), math.log(1.8)))
    base = jax.random.normal(base_key, (SEQS, LEN, D), jnp.float32)
    base = jnp.clip(base, -4.0, 4.0)
    return (base * row_scale * col_scale).astype(jnp.bfloat16)


def draw_seq_ids(key, part):
    key = jax.random.fold_in(key, 23)
    head_key, tail_key = jax.random.split(key)
    reach = min(32, TOK_DEV)
    head_end = jax.random.randint(head_key, (SEQS, 1), 1, reach)
    tail_start = LEN - jax.random.randint(tail_key, (SEQS, 1), 1, reach)
    positions = jnp.arange(LEN, dtype=jnp.int32)[None, :]
    return (positions >= head_end).astype(jnp.int32) + (positions >= tail_start).astype(jnp.int32)


def plant(values, stream_key, least, high):
    extent = values.shape
    place = [jax.random.randint(jax.random.fold_in(stream_key, axis), (), 0, extent[axis]) for axis in range(len(extent))]
    values = values.at[tuple(place)].set(least)
    longest = extent.index(max(extent))
    place[longest] = (place[longest] + 1) % extent[longest]
    return values.at[tuple(place)].set(high)


def levels(stream_key, extent, cuts, smallest, top_value):
    def one(position, blocks):
        steps = jax.random.uniform(jax.random.fold_in(jax.random.fold_in(stream_key, 6), position), (blocks,), jnp.float32, smallest / len(cuts), top_value / len(cuts))
        return jnp.repeat(jnp.exp(steps), extent[position] // blocks).reshape((-1,) + (1,) * (len(extent) - position - 1))

    factor_of = one(*cuts[0])
    for cut in cuts[1:]:
        factor_of = factor_of * one(*cut)
    return factor_of


def shared_out(key, own, number, rows, amount, top, bound, skew):
    order = jax.random.permutation(key, amount)
    packed, common = portions_of(amount, rows * top, bound, skew, True), portions_of(amount, rows * top, bound, skew, False)
    places = jnp.arange(amount)

    def named(lengths, rotation):
        used = int((lengths > 0).sum())
        fixed = max(1, used // 4)
        passed = fixed + (places - fixed + rotation * (used - fixed)) % max(1, amount - fixed)
        return jnp.zeros((amount,), jnp.int32).at[order[jnp.where(places < fixed, places, passed)]].set(jnp.asarray(lengths, jnp.int32))

    lengths = jnp.where(number % 4 == 0, named(packed, number // 4), named(common, number - number // 4 - 1))
    mixed = jax.random.permutation(jax.random.fold_in(own, 3), amount)
    giver, taker = mixed[0:amount // 2 * 2:2], mixed[1:amount // 2 * 2:2]
    room = jnp.minimum(lengths[giver] - 1, bound - lengths[taker]) // 2
    room = jnp.where((giver == order[0]) | (taker == order[0]) | (lengths[taker] == 0), 0, jnp.maximum(room, 0))
    passed = jax.random.randint(jax.random.fold_in(own, 4), (amount // 2,), 0, 1 << 20) % (room + 1)
    lengths = lengths.at[giver].add(-passed).at[taker].add(passed)
    members = jnp.searchsorted(jnp.cumsum(lengths), jnp.arange(rows * top), side="right").astype(jnp.int32)
    grid = members.reshape(top, rows).T
    grid = grid[jax.random.permutation(jax.random.fold_in(own, 1), rows)]
    rotation = jax.random.randint(jax.random.fold_in(own, 2), (rows, 1), 0, top)
    return jnp.take_along_axis(grid, (jnp.arange(top)[None, :] + rotation) % top, axis=1)


def portions_of(count, total, most, slope, full):
    loads = [(1 << 20) // math.isqrt(standing ** slope) + 1 for standing in range(1, count + 1)]
    largest = most if full else min(most, max(-(-total // count), total * loads[0] // sum(loads)))
    least = 1 if total - largest >= count - 1 else 0
    holding, surplus = [largest] + [least] * (count - 1), total - largest - least * (count - 1)
    while surplus > 0:
        free = [i for i in range(1, count) if holding[i] < largest] or [i for i in range(1, count) if holding[i] < most]
        whole, left = sum([loads[i] for i in free]), surplus
        for i in free:
            extra = min(most - holding[i], max(1, left * loads[i] // whole), surplus)
            holding[i] = holding[i] + extra
            surplus = surplus - extra
    return np.array(holding)


def scatter_about(own_key, extent, spread, most, shards=(), kind=jnp.bfloat16):
    factor_of = levels(own_key, extent, shards, -0.22, 0.18) if shards else 1.0
    values = jax.random.normal(own_key, extent, jnp.float32) * spread * factor_of
    return jnp.minimum(jnp.maximum(values, -most), most).astype(kind)


def setup_inputs(seed: int = 0) -> dict:
    key_list = jax.random.split(jax.random.key(seed), 16)
    tokens = draw_tokens(jax.random.fold_in(key_list[15], 71), 0)
    w_query = scatter_about(key_list[1], (D, D), D ** -0.5, 0.21875, ((0, 8),))
    w_key = scatter_about(key_list[2], (D, D), D ** -0.5, 0.21875, ((0, 8),))
    w_value = scatter_about(key_list[3], (D, D), D ** -0.5, 0.21875, ((0, 8),))
    w_output = scatter_about(key_list[4], (D, D), (max(D // 128, 1)) ** -0.5, 2.5, ((0, 8),))
    w_router = scatter_about(key_list[5], (D, EXPERTS), (2 * D) ** -0.5, 0.15625, ((0, 8),))
    norm_one = jnp.clip(1.0 + 0.1 * jax.random.normal(key_list[6], (D,), jnp.float32), 0.5, 1.5).astype(jnp.bfloat16)
    norm_two = jnp.clip(1.0 + 0.1 * jax.random.normal(key_list[7], (D,), jnp.float32), 0.5, 1.5).astype(jnp.bfloat16)
    rel_bias = scatter_about(key_list[8], (NB, H), 1.0, 4.0, ((0, 8),))
    w_in = scatter_about(key_list[9], (EXPERTS, D, FF), D ** -0.5, 0.21875, ((0, 4),))
    w_out = scatter_about(key_list[10], (EXPERTS, FF, D), (max(FF // 160, 1)) ** -0.5, 1.25, ((0, 4),))
    routes_keys = jax.random.split(jax.random.fold_in(key_list[11], 1), SEQS * LEN // TOK_DEV)
    routes_turns = jax.random.permutation(jax.random.fold_in(key_list[11], 3), SEQS * LEN // TOK_DEV)
    routes = jax.vmap(lambda own, number: shared_out(jax.random.fold_in(key_list[11], 2), own, number, TOK_DEV, EXPERTS, 1, CAP, 2))(routes_keys, routes_turns).reshape((SEQS, LEN, 1))
    seq_ids = draw_seq_ids(jax.random.fold_in(key_list[15], 71), 0)
    buckets = plant(jax.random.randint(key_list[13], (2 * LEN - 1,), 0, NB), jax.random.fold_in(key_list[13], 1), 0, NB - 1).astype(jnp.int32)
    d_out = scatter_about(key_list[14], (SEQS, LEN, D), 1.0, 6.0, ((0, 8), (1, 4)))
    return dict(tokens=tokens, w_query=w_query, w_key=w_key, w_value=w_value, w_output=w_output, w_router=w_router, norm_one=norm_one, norm_two=norm_two, rel_bias=rel_bias, w_in=w_in, w_out=w_out, routes=routes, seq_ids=seq_ids, buckets=buckets, d_out=d_out)


@jax.custom_vjp
def low(v):
    return lax.optimization_barrier(v.astype(jnp.bfloat16)).astype(jnp.float32)

@jax.custom_vjp
def low_back(v):
    return v

def low_keep(v):
    return (low(v), None)

def low_pass(kept, grad):
    return (grad,)

def back_keep(v):
    return (v, None)

def back_low(kept, grad):
    return (low(grad),)
low.defvjp(low_keep, low_pass)
low_back.defvjp(back_keep, back_low)
EPSILON = 1e-06
NEGATIVE = -1e+30
HIGHEST = lax.Precision.HIGHEST

def rounded(values_in):
    return low(low_back(values_in))

def matmul(left, right):
    return jnp.dot(left, right, precision=HIGHEST)

def rms_norm(values_in, gain):
    inverse = lax.rsqrt(lax.optimization_barrier(jnp.mean(values_in * values_in, axis=-1, keepdims=True)) + EPSILON)
    return values_in * inverse * gain

@jax.checkpoint
def attend_block(query_heads, row_start, key_heads, value_heads, seq_row, bias_table, buckets):
    block_rows = query_heads.shape[0]
    positions = row_start + jnp.arange(block_rows, dtype=jnp.int32)
    columns = jnp.arange(LEN, dtype=jnp.int32)
    offsets = columns[None, :] - positions[:, None] + (LEN - 1)
    score_bias = jnp.transpose(bias_table[buckets[offsets]], (2, 0, 1))
    raw_scores = low_back(jnp.einsum('qhd,khd->hqk', query_heads, key_heads, precision=HIGHEST))
    scores = raw_scores * HD ** (-0.5) + score_bias
    query_ids = lax.dynamic_slice_in_dim(seq_row, row_start, block_rows)
    same_doc = query_ids[:, None] == seq_row[None, :]
    scores = jnp.where(same_doc[None], scores, NEGATIVE)
    row_peak = lax.optimization_barrier(jnp.max(scores, axis=-1, keepdims=True))
    exponent = jnp.exp(scores - row_peak)
    weights = low(exponent / lax.optimization_barrier(jnp.sum(exponent, axis=-1, keepdims=True)))
    return jnp.einsum('hqk,khd->qhd', weights, value_heads, precision=HIGHEST)

def attend_sequence(queries, keys, values, seq_row, bias_table, buckets):
    block_count = max(1, LEN // 512)
    block_rows = LEN // block_count
    key_heads = keys.reshape(LEN, H, HD)
    value_heads = values.reshape(LEN, H, HD)
    starts = jnp.arange(block_count, dtype=jnp.int32) * block_rows
    query_blocks = queries.reshape(block_count, block_rows, H, HD)

    def one_block(item):
        return attend_block(item[0], item[1], key_heads, value_heads, seq_row, bias_table, buckets)
    mixed = lax.map(one_block, (query_blocks, starts))
    return mixed.reshape(LEN, D)

@jax.checkpoint
def expert_rows(entry, weight_a, weight_b, chosen_rows):
    pre_act = low_back(matmul(entry, weight_a))
    activated = low(jax.nn.gelu(pre_act, approximate=True))
    return jnp.where(chosen_rows[:, None], rounded(matmul(activated, weight_b)), 0.0)

def layer(tokens, w_query, w_key, w_value, w_output, w_router, norm_one, norm_two, rel_bias, w_in, w_out, routes, seq_ids, buckets):
    flat_rows = tokens.reshape(SEQS * LEN, D)
    h_one = low(rms_norm(flat_rows, norm_one))
    queries = rounded(matmul(h_one, w_query))
    keys = rounded(matmul(h_one, w_key))
    values = rounded(matmul(h_one, w_value))

    def one_sequence(item):
        return attend_sequence(item[0], item[1], item[2], item[3], rel_bias, buckets)
    mixed = lax.map(one_sequence, (queries.reshape(SEQS, LEN, D), keys.reshape(SEQS, LEN, D), values.reshape(SEQS, LEN, D), seq_ids))
    attended = rounded(mixed.reshape(SEQS * LEN, D))
    x_one = flat_rows + low_back(matmul(attended, w_output))
    h_two = low(rms_norm(x_one, norm_two))
    router_probs = jax.nn.softmax(matmul(h_two, w_router), axis=-1)
    route_ids = routes.reshape(SEQS * LEN)
    chosen = route_ids[:, None] == jnp.arange(EXPERTS, dtype=jnp.int32)[None, :]
    gate_value = lax.optimization_barrier(jnp.sum(jnp.where(chosen, router_probs, 0.0), axis=1, keepdims=True))
    entry = low_back(h_two)

    def add_expert(running, item):
        return (running + expert_rows(entry, item[0], item[1], route_ids == item[2]), None)
    expert_out, _ = lax.scan(add_expert, jnp.zeros_like(flat_rows), (w_in, w_out, jnp.arange(EXPERTS, dtype=jnp.int32)))
    return (x_one + gate_value * expert_out).reshape(SEQS, LEN, D)

def reference(tokens, w_query, w_key, w_value, w_output, w_router, norm_one, norm_two, rel_bias, w_in, w_out, routes, seq_ids, buckets, d_out):
    params = [array.astype(jnp.float32) for array in (tokens, w_query, w_key, w_value, w_output, w_router, norm_one, norm_two, rel_bias, w_in, w_out)]

    def forward(*inputs):
        return layer(*inputs, routes, seq_ids, buckets)
    result, pullback = jax.vjp(forward, *params)
    grads = pullback(d_out.astype(jnp.float32))
    return (result.astype(jnp.bfloat16), grads[0], grads[1], grads[2], grads[3], grads[4], grads[5], grads[6], grads[7], grads[8], grads[9], grads[10])
```

```python
import jax
import jax.numpy as jnp
from jax import lax
from jax.experimental import pallas as pl
from jax.experimental.pallas import tpu as pltpu
from jax.sharding import PartitionSpec as P

H = 12
HD = 64

EPSILON = 1e-06
NEGATIVE = -1e30
HIGHEST = lax.Precision.HIGHEST


def product(left, right):
    return jnp.dot(left, right, preferred_element_type=jnp.float32)


def contract(left, right, left_dim, right_dim):
    return lax.dot_general(
        left, right, (((left_dim,), (right_dim,)), ((), ())), preferred_element_type=jnp.float32
    )


def norm_forward(values_in, gain):
    inverse = lax.rsqrt(jnp.mean(values_in * values_in, axis=-1, keepdims=True) + EPSILON)
    return (values_in * inverse * gain, inverse)


def norm_backward(values_in, inverse, gain, grad_in):
    scaled = grad_in * gain
    inner_mean = jnp.mean(scaled * values_in, axis=-1, keepdims=True)
    grad_out = inverse * scaled - values_in * (inverse * inverse * inverse) * inner_mean
    gain_grad = jnp.sum(grad_in * values_in * inverse, axis=0)
    return (grad_out, gain_grad)


def round_up(count, step):
    return -(-count // step) * step


def block_scores(query_ref, key_ref, row_ids_ref, col_ids_ref, window_ref):
    rows = query_ref.shape[1]
    length = key_ref.shape[1]
    span = window_ref.shape[3]
    spread = jnp.broadcast_to(window_ref[0, 0], (rows, span))
    bias = pltpu.roll(spread, span - (rows - 1), 1, stride=1, stride_axis=0)[:, :length]
    scores = contract(query_ref[0], key_ref[0], 1, 1) + bias
    return jnp.where(row_ids_ref[...] == col_ids_ref[...], scores, NEGATIVE)


def forward_kernel(
    query_ref, key_ref, value_ref, row_ids_ref, col_ids_ref, window_ref, mixed_ref, log_ref
):
    scores = block_scores(query_ref, key_ref, row_ids_ref, col_ids_ref, window_ref)
    peak = jnp.max(scores, axis=1, keepdims=True)
    powers = jnp.exp(scores - peak)
    total = jnp.sum(powers, axis=1, keepdims=True)
    weights = (powers * (1.0 / total)).astype(jnp.bfloat16)
    mixed_ref[0] = contract(weights, value_ref[0], 1, 0)
    log_ref[0] = peak + jnp.log(total)


def backward_kernel(
    query_ref,
    key_ref,
    value_ref,
    row_ids_ref,
    col_ids_ref,
    window_ref,
    mixed_ref,
    log_ref,
    d_mixed_ref,
    d_query_ref,
    d_key_ref,
    d_value_ref,
    d_window_ref,
):
    rows = query_ref.shape[1]
    length = key_ref.shape[1]
    span = window_ref.shape[3]

    @pl.when(pl.program_id(1) == 0)
    def _():
        d_key_ref[...] = jnp.zeros_like(d_key_ref)
        d_value_ref[...] = jnp.zeros_like(d_value_ref)

    scores = block_scores(query_ref, key_ref, row_ids_ref, col_ids_ref, window_ref)
    weights = jnp.exp(scores - log_ref[0])
    d_mixed = d_mixed_ref[0]
    delta = jnp.sum(d_mixed.astype(jnp.float32) * mixed_ref[0], axis=1, keepdims=True)
    d_scores = weights * (contract(d_mixed, value_ref[0], 1, 1) - delta)
    d_low = d_scores.astype(jnp.bfloat16)
    d_query_ref[0] = (contract(d_low, key_ref[0], 1, 0) * (HD**-0.5)).astype(jnp.bfloat16)
    d_key_ref[0] += contract(d_low, query_ref[0], 0, 0)
    d_value_ref[0] += contract(weights.astype(jnp.bfloat16), d_mixed, 0, 0)
    folded = jnp.concatenate(
        [d_scores, jnp.zeros((rows, span - length), jnp.float32)], axis=1
    )
    half = rows // 2
    while half >= 8:
        folded = pltpu.roll(folded[:half], half, 1) + folded[half:]
        half //= 2
    d_window_ref[0, 0] = folded


def attention_specs(heads, blocks, rows, length, span):
    per_block = pl.BlockSpec((1, rows, HD), lambda h, i: (h, i, 0))
    per_head = pl.BlockSpec((1, length, HD), lambda h, i: (h, 0, 0))
    row_ids = pl.BlockSpec((rows, 1), lambda h, i: (i, 0))
    col_ids = pl.BlockSpec((1, length), lambda h, i: (0, 0))
    window = pl.BlockSpec((1, 1, 1, span), lambda h, i: (h, i, 0, 0))
    logs = pl.BlockSpec((1, rows, 1), lambda h, i: (h, i, 0))
    return per_block, per_head, row_ids, col_ids, window, logs


def attention_forward(query, key, value, row_ids, col_ids, windows):
    heads, length, _ = query.shape
    blocks, span = windows.shape[1], windows.shape[3]
    rows = length // blocks
    per_block, per_head, rid, cid, window, logs = attention_specs(
        heads, blocks, rows, length, span
    )
    return pl.pallas_call(
        forward_kernel,
        grid=(heads, blocks),
        in_specs=[per_block, per_head, per_head, rid, cid, window],
        out_specs=[per_block, logs],
        out_shape=[
            jax.ShapeDtypeStruct((heads, length, HD), jnp.float32),
            jax.ShapeDtypeStruct((heads, length, 1), jnp.float32),
        ],
        compiler_params=pltpu.CompilerParams(vmem_limit_bytes=40 * 1024 * 1024),
        cost_estimate=pl.CostEstimate(
            flops=4 * heads * length * length * HD,
            bytes_accessed=heads * length * HD * 12,
            transcendentals=heads * length * length,
        ),
        name="attention_forward",
    )(query, key, value, row_ids, col_ids, windows)


def attention_backward(query, key, value, row_ids, col_ids, windows, mixed, logs_in, d_mixed):
    heads, length, _ = query.shape
    blocks, span = windows.shape[1], windows.shape[3]
    rows = length // blocks
    per_block, per_head, rid, cid, window, logs = attention_specs(
        heads, blocks, rows, length, span
    )
    return pl.pallas_call(
        backward_kernel,
        grid=(heads, blocks),
        in_specs=[
            per_block, per_head, per_head, rid, cid, window, per_block, logs, per_block,
        ],
        out_specs=[
            per_block,
            per_head,
            per_head,
            pl.BlockSpec((1, 1, 8, span), lambda h, i: (h, i, 0, 0)),
        ],
        out_shape=[
            jax.ShapeDtypeStruct((heads, length, HD), jnp.bfloat16),
            jax.ShapeDtypeStruct((heads, length, HD), jnp.float32),
            jax.ShapeDtypeStruct((heads, length, HD), jnp.float32),
            jax.ShapeDtypeStruct((heads, blocks, 8, span), jnp.float32),
        ],
        compiler_params=pltpu.CompilerParams(vmem_limit_bytes=40 * 1024 * 1024),
        cost_estimate=pl.CostEstimate(
            flops=10 * heads * length * length * HD,
            bytes_accessed=heads * length * HD * 24,
            transcendentals=heads * length * length,
        ),
        name="attention_backward",
    )(query, key, value, row_ids, col_ids, windows, mixed, logs_in, d_mixed)


def swap_parts(values_in, axis):
    return lax.all_to_all(values_in, axis, split_axis=0, concat_axis=0, tiled=True)


def head_major(rows_in, heads):
    return jnp.transpose(rows_in.reshape(rows_in.shape[0], heads, HD), (1, 0, 2))


def row_major(heads_in):
    heads, length, _ = heads_in.shape
    return jnp.transpose(heads_in, (1, 0, 2)).reshape(length, heads * HD)


def per_device(
    tokens,
    w_query,
    w_key,
    w_value,
    w_output,
    w_router,
    norm_one,
    norm_two,
    rel_bias,
    w_in,
    w_out,
    routes,
    seq_ids,
    buckets,
    d_out,
):
    low = jnp.bfloat16
    members = lax.axis_size("expert")
    shards = lax.axis_size("shard")
    me = lax.axis_index("expert")
    row_count = tokens.shape[1]
    width = tokens.shape[2]
    length = row_count * members
    part_rows = w_query.shape[0]
    table_rows, experts = rel_bias.shape[0], w_router.shape[1]
    heads = -(-H // members)
    lanes = heads * HD
    extra = members * lanes - width

    def own_columns(weight):
        return lax.dynamic_slice_in_dim(
            jnp.pad(weight, ((0, 0), (0, extra))), me * lanes, lanes, 1
        )

    used = 3 * lanes + 2 + experts + H
    packed = jnp.concatenate(
        [
            own_columns(w_query),
            own_columns(w_key),
            own_columns(w_value),
            norm_one[:, None],
            norm_two[:, None],
            w_router,
            jnp.pad(rel_bias, ((0, part_rows - table_rows), (0, 0))),
            jnp.zeros((part_rows, round_up(used, 128) - used), low),
        ],
        axis=1,
    )
    gathered = lax.all_gather(packed, "shard", axis=0, tiled=True)
    rows_all = lax.all_gather(tokens[0], "expert", axis=0, tiled=True)
    output_all = lax.all_gather(w_output, "shard", axis=0, tiled=True)
    weights_qkv = gathered[:, : 3 * lanes]
    at = 3 * lanes
    gain_one_f = gathered[:, at].astype(jnp.float32)
    gain_two_f = gathered[:, at + 1].astype(jnp.float32)
    router_all = gathered[:, at + 2 : at + 2 + experts]
    table_all = gathered[:, at + 2 + experts : used].reshape(shards, part_rows, H)[:, :table_rows]
    table_all = jnp.pad(
        table_all.reshape(shards * table_rows, H), ((0, 0), (0, members * heads - H))
    )
    table_own = lax.dynamic_slice_in_dim(table_all, me * heads, heads, 1)

    flat_rows = tokens[0].astype(jnp.float32)
    h_all, _ = norm_forward(rows_all.astype(jnp.float32), gain_one_f)
    h_all_low = h_all.astype(low)
    qkv = product(h_all_low, weights_qkv).astype(low)
    query = head_major(qkv[:, :lanes] * jnp.asarray(HD**-0.5, low), heads)
    key = head_major(qkv[:, lanes : 2 * lanes], heads)
    value = head_major(qkv[:, 2 * lanes :], heads)
    row_ids = seq_ids[0][:, None]
    col_ids = seq_ids
    bucket_hot = buckets[:, None] == jnp.arange(table_all.shape[0], dtype=jnp.int32)[None, :]
    offset_bias = contract(table_own, bucket_hot.astype(low), 0, 1)
    block = 256 if length % 256 == 0 else length
    blocks = length // block
    span = block + length
    offset_padded = jnp.pad(offset_bias, ((0, 0), (0, 1)))
    windows = jnp.stack(
        [
            offset_padded[:, length - (i + 1) * block : 2 * length - i * block]
            for i in range(blocks)
        ],
        axis=1,
    )[:, :, None, :]
    mixed, log_total = attention_forward(query, key, value, row_ids, col_ids, windows)
    mixed_low = row_major(mixed.astype(low)).reshape(members, row_count, lanes)
    attn_low = jnp.transpose(swap_parts(mixed_low, "expert"), (1, 0, 2)).reshape(
        row_count, members * lanes
    )[:, :width]

    x_one = flat_rows + product(attn_low, output_all)
    h_two, inverse_two = norm_forward(x_one, gain_two_f)
    h_two_low = h_two.astype(low)
    router_probs = jax.nn.softmax(product(h_two_low, router_all), axis=-1)
    route_ids = routes[0, :, 0]
    chosen_int = (route_ids[:, None] == jnp.arange(experts, dtype=jnp.int32)[None, :]).astype(
        jnp.int32
    )
    chosen = chosen_int.astype(jnp.float32)
    gate_value = jnp.sum(router_probs * chosen, axis=1)
    capacity = 2 * row_count // experts
    rank_index = jnp.sum((jnp.cumsum(chosen_int, axis=0) - chosen_int) * chosen_int, axis=1)
    slot_index = route_ids * capacity + rank_index
    slots = experts * capacity
    placement = (
        jnp.arange(slots, dtype=jnp.int32)[:, None] == slot_index[None, :]
    ).astype(low)
    d_two = d_out[0].astype(jnp.float32)
    d_result = (gate_value[:, None] * d_two).astype(low)
    send = product(placement, jnp.concatenate([h_two_low, d_result], axis=1)).astype(low)
    arrived = swap_parts(send.reshape(experts, capacity, 2 * width), "expert").reshape(
        slots, 2 * width
    )
    received, d_received = arrived[:, :width], arrived[:, width:]
    pre_act = product(received, w_in[0])
    act, gelu_back = jax.vjp(lambda u: jax.nn.gelu(u, approximate=True), pre_act)
    act_low = act.astype(low)
    result_rows = product(act_low, w_out[0]).astype(low)
    d_act = contract(d_received, w_out[0], 1, 1)
    d_pre = gelu_back(d_act)[0].astype(low)
    d_entry = contract(d_pre, w_in[0], 1, 1).astype(low)
    back = swap_parts(
        jnp.concatenate([result_rows, d_entry], axis=1).reshape(experts, capacity, 2 * width),
        "expert",
    ).reshape(slots, 2 * width)
    d_w_out_part = contract(act_low, d_received, 0, 0).astype(low)
    d_w_in_part = contract(received, d_pre, 0, 0).astype(low)
    landed = contract(placement, back, 0, 0)
    expert_out, d_h_two = landed[:, :width], landed[:, width:]
    layer_out = (x_one + gate_value[:, None] * expert_out).astype(low)
    d_gate = jnp.sum(d_two * expert_out, axis=1)
    d_logits = router_probs * (chosen * d_gate[:, None] - (gate_value * d_gate)[:, None])
    d_router = jnp.dot(h_two_low.astype(jnp.float32).T, d_logits, precision=HIGHEST)
    d_h_two = d_h_two + jnp.dot(d_logits, router_all.astype(jnp.float32).T, precision=HIGHEST)
    d_x_part, d_gain_two = norm_backward(x_one, inverse_two, gain_two_f, d_h_two)
    d_x_one = d_two + d_x_part
    d_branch = d_x_one.astype(low)
    d_output = contract(attn_low, d_branch, 0, 0).astype(low)
    d_attn = contract(d_branch, output_all, 1, 1).astype(low)

    fold = w_out.shape[1] // width
    d_w_out_folded = jnp.transpose(
        d_w_out_part.reshape(shards, fold, part_rows, width), (0, 2, 1, 3)
    ).reshape(width, fold * width)
    early_used = experts + 1
    early = jnp.concatenate(
        [
            d_w_in_part,
            d_w_out_folded,
            d_output,
            d_router.astype(low),
            d_gain_two.astype(low)[:, None],
            jnp.zeros((width, round_up(early_used, 128) - early_used), low),
        ],
        axis=1,
    )
    early, d_attn = lax.optimization_barrier((early, d_attn))
    early_sum = lax.psum_scatter(early, "shard", scatter_dimension=0, tiled=True)

    d_attn_parts = jnp.transpose(
        jnp.pad(d_attn, ((0, 0), (0, extra))).reshape(row_count, members, lanes), (1, 0, 2)
    )
    d_mixed = head_major(swap_parts(d_attn_parts, "expert").reshape(length, lanes), heads)
    d_query, d_key, d_value, d_windows = attention_backward(
        query, key, value, row_ids, col_ids, windows, mixed, log_total, d_mixed
    )
    d_qkv = jnp.concatenate(
        [row_major(d_query), row_major(d_key.astype(low)), row_major(d_value.astype(low))], axis=1
    )
    d_h_parts = contract(d_qkv, weights_qkv, 1, 1).astype(low)
    d_h_one = jnp.sum(
        swap_parts(d_h_parts.reshape(members, row_count, width), "expert").astype(jnp.float32),
        axis=0,
    )
    d_w_qkv = contract(h_all_low, d_qkv, 0, 0).astype(low)
    d_window = sum(
        jnp.pad(d_windows[:, :, r, : span - (7 - r)], ((0, 0), (0, 0), (7 - r, 0)))
        for r in range(8)
    )
    d_offsets = sum(
        jnp.pad(
            d_window[:, i],
            ((0, 0), (length - (i + 1) * block, i * block)),
        )
        for i in range(blocks)
    )[:, : 2 * length - 1]
    d_table = jnp.einsum(
        "ob,ho->bh", bucket_hot.astype(jnp.float32), d_offsets, precision=HIGHEST
    )
    inverse_one = lax.rsqrt(jnp.mean(flat_rows * flat_rows, axis=-1, keepdims=True) + EPSILON)
    d_x_first, d_gain_one = norm_backward(flat_rows, inverse_one, gain_one_f, d_h_one)
    d_tokens = (d_x_one + d_x_first)[None]

    late_used = 3 * lanes + 1 + heads
    d_table_rows = jnp.pad(
        d_table.astype(low).reshape(shards, table_rows, heads),
        ((0, 0), (0, part_rows - table_rows), (0, 0)),
    ).reshape(width, heads)
    late = jnp.concatenate(
        [
            d_w_qkv,
            d_gain_one.astype(low)[:, None],
            d_table_rows,
            jnp.zeros((width, round_up(late_used, 128) - late_used), low),
        ],
        axis=1,
    )
    late_sum = jnp.sum(
        swap_parts(late.reshape(shards, part_rows, late.shape[1]), "shard").astype(jnp.float32),
        axis=0,
    ).astype(low)
    both = jnp.concatenate([late_sum, early_sum[:, 2 * w_in.shape[2] :]], axis=1)
    all_parts = lax.all_gather(both, "expert", axis=0, tiled=False).astype(jnp.float32)

    def joined(start, size):
        taken = all_parts[:, :, start : start + size]
        return jnp.transpose(taken, (1, 0, 2)).reshape(part_rows, members * size)

    late_width = late.shape[1]
    total_q = joined(0, lanes)[:, :width]
    total_k = joined(lanes, lanes)[:, :width]
    total_v = joined(2 * lanes, lanes)[:, :width]
    total_one = jnp.sum(all_parts[:, :, 3 * lanes], axis=0)
    total_table = joined(3 * lanes + 1, heads)[:table_rows, :H]
    summed = jnp.sum(all_parts[:, :, late_width:], axis=0)
    total_o = summed[:, :width]
    total_router = summed[:, width : width + experts]
    total_two = summed[:, width + experts]
    ff = w_in.shape[2]
    grad_in = early_sum[:, :ff].astype(jnp.float32)[None]
    grad_out = jnp.transpose(
        early_sum[:, ff : 2 * ff].reshape(part_rows, fold, width), (1, 0, 2)
    ).reshape(1, fold * part_rows, width).astype(jnp.float32)
    return (
        layer_out[None],
        d_tokens,
        total_q,
        total_k,
        total_v,
        total_o,
        total_router,
        total_one,
        total_two,
        total_table,
        grad_in,
        grad_out,
    )


def solution(mesh):
    placed = (
        P("shard", "expert", None),
        P("shard", None),
        P("shard", None),
        P("shard", None),
        P("shard", None),
        P("shard", None),
        P("shard"),
        P("shard"),
        P("shard", None),
        P("expert", None, None),
        P("expert", None, None),
        P("shard", "expert", None),
        P("shard", None),
        P(),
        P("shard", "expert", None),
    )
    return jax.shard_map(
        per_device,
        mesh=mesh,
        in_specs=placed,
        out_specs=(
            P("shard", "expert", None),
            P("shard", "expert", None),
            P("shard", None),
            P("shard", None),
            P("shard", None),
            P("shard", None),
            P("shard", None),
            P("shard"),
            P("shard"),
            P("shard", None),
            P("expert", "shard", None),
            P("expert", "shard", None),
        ),
        check_vma=False,
    )
```
